1024 devices in a mesh: dp: 128 (over z_hi, x, y, core), expert: 8 (over z_lo).
Axes of the slice: x: 4, y: 8, z: 16 (z_hi: 2, z_lo: 8; z = z_hi * 8 + z_lo), core: 2. Of those that a mesh axis runs over, the one named last changes fastest.
Arguments:
- picture_vectors: bfloat16 [393216, 1024], P(('dp', 'expert')), may hold values from -1 to 1
- caption_vectors: bfloat16 [65536, 1024], P(('dp', 'expert')), may hold values from -1 to 1
- projector_inputs: bfloat16 [393216, 640], P(('dp', 'expert')), may hold values from -0.017944336 to 0.017944336
- assigned_specialist: int32 [393216, 1], P(('dp', 'expert')), may hold values from 0 to 7; in each aligned block of 384 rows (0 to 383, 384 to 767, ...) at most 60 rows name the same one
- score_multiplier: float32 [1], replicated, may hold values from 1 to 4
- score_shift: float32 [1], replicated, may hold values from -2 to 0
Outputs:
- image_loss: float32 [393216], P(('dp', 'expert'))
- text_grad: float32 [65536, 1024], P(('dp', 'expert'))
- expert_grad: float32 [8, 1024, 640], P('expert', 'dp')
The draws below stay inside these ranges and needn't reach their ends.
Inputs may be any that keep to these rules, and one draw needn't show every extreme that they name: `assigned_specialist`: among the images of one device at most 60 name any one expert, and in every draw some expert is named by exactly 60 of them on some device; every expert is named somewhere.
All inputs are finite; a program needn't handle non-finite values.
Results may differ from the reference program's by a relative error of at most 0.0037.
Values may be sent and summed in bfloat16 or wider, within the bound.
A program may use at most 32 MiB of HBM per device.

```python
import math
import jax
import jax.numpy as jnp
import numpy as np
from jax import lax

E = 1024
DXW = 640
STEPS = 4
TXT_DEV = 64
IMG_DEV = 384
EXPERTS = 8
CAP = 60
IMAGES = 393216
TEXTS = 65536
N_DP = 128
N_EXPERT = 8


def shard_levels(stream_key, extent, shards, least, high):
    level = 1.0
    for axis_at, blocks in shards:
        draws = jax.random.uniform(jax.random.fold_in(jax.random.fold_in(stream_key, 6), axis_at), (blocks,), jnp.float32, least / len(shards), high / len(shards))
        level = level * jnp.repeat(jnp.exp(draws), extent[axis_at] // blocks).reshape((-1,) + (1,) * (len(extent) - 1 - axis_at))
    return level


def assign_block(stream_key, own, number, rows, count, top, limit, skew):
    order = jax.random.permutation(stream_key, count)
    heavy_load, ordinary = portions_of(count, rows * top, limit, skew, True), portions_of(count, rows * top, limit, skew, False)
    places = jnp.arange(count)

    def named(tallies, rotation):
        used = int((tallies > 0).sum())
        fixed = max(1, used // 4)
        shifted = fixed + (places - fixed + rotation * (used - fixed)) % max(1, count - fixed)
        return jnp.zeros((count,), jnp.int32).at[order[jnp.where(places < fixed, places, shifted)]].set(jnp.asarray(tallies, jnp.int32))

    tallies = jnp.where(number % 4 == 0, named(heavy_load, number // 4), named(ordinary, number - number // 4 - 1))
    mixed = jax.random.permutation(jax.random.fold_in(own, 3), count)
    donor, sink = mixed[0:count // 2 * 2:2], mixed[1:count // 2 * 2:2]
    slack = jnp.minimum(tallies[donor] - 1, limit - tallies[sink]) // 2
    slack = jnp.where((donor == order[0]) | (sink == order[0]) | (tallies[sink] == 0), 0, jnp.maximum(slack, 0))
    shifted = jax.random.randint(jax.random.fold_in(own, 4), (count // 2,), 0, 1 << 20) % (slack + 1)
    tallies = tallies.at[donor].add(-shifted).at[sink].add(shifted)
    labels = jnp.searchsorted(jnp.cumsum(tallies), jnp.arange(rows * top), side="right").astype(jnp.int32)
    listing = labels.reshape(top, rows).T
    listing = listing[jax.random.permutation(jax.random.fold_in(own, 1), rows)]
    rotation = jax.random.randint(jax.random.fold_in(own, 2), (rows, 1), 0, top)
    return jnp.take_along_axis(listing, (jnp.arange(top)[None, :] + rotation) % top, axis=1)


def portions_of(number_of, total, most, slope, full):
    loads = [(1 << 20) // math.isqrt(rank ** slope) + 1 for rank in range(1, number_of + 1)]
    largest = most if full else min(most, max(-(-total // number_of), total * loads[0] // sum(loads)))
    least = 1 if total - largest >= number_of - 1 else 0
    holding, spare = [largest] + [least] * (number_of - 1), total - largest - least * (number_of - 1)
    while spare > 0:
        candidates = [i for i in range(1, number_of) if holding[i] < largest] or [i for i in range(1, number_of) if holding[i] < most]
        pool, budget = sum([loads[i] for i in candidates]), spare
        for i in candidates:
            addition = min(most - holding[i], max(1, budget * loads[i] // pool), spare)
            holding[i] = holding[i] + addition
            spare = spare - addition
    return np.array(holding)


def normal_values(rng, extent, deviation, reach, split=(), kind=jnp.bfloat16):
    values = deviation * jax.random.normal(rng, extent, jnp.float32)
    if split:
        values = values * shard_levels(rng, extent, split, -0.22, 0.18)
    return jnp.clip(values, -reach, reach).astype(kind)


def setup_inputs(seed: int = 0) -> dict:
    key_of = jax.random.split(jax.random.key(seed), 7)
    picture_vectors = normal_values(key_of[0], (IMAGES, E), 0.18, 1.0, ((0, 1024),))
    caption_vectors = normal_values(key_of[1], (TEXTS, E), 0.18, 1.0, ((0, 1024),))
    projector_inputs = normal_values(key_of[2], (IMAGES, DXW), 0.003, 0.017944336, ((0, 1024),))
    assigned_specialist_keys = jax.random.split(jax.random.fold_in(key_of[3], 1), IMAGES // IMG_DEV)
    assigned_specialist_turns = jax.random.permutation(jax.random.fold_in(key_of[3], 3), IMAGES // IMG_DEV)
    assigned_specialist = jax.vmap(lambda own, number: assign_block(jax.random.fold_in(key_of[3], 2), own, number, IMG_DEV, EXPERTS, 1, CAP, 2))(assigned_specialist_keys, assigned_specialist_turns).reshape((IMAGES, 1))
    score_multiplier = jnp.clip(jnp.exp(jax.random.uniform(key_of[4], (1,), jnp.float32, math.log(1.0), math.log(4.0))), 1.0, 4.0)
    score_shift = jnp.clip(jax.random.uniform(key_of[5], (1,), jnp.float32, -2.0, 0.0), -2.0, 0.0)
    return {"picture_vectors": picture_vectors, "caption_vectors": caption_vectors, "projector_inputs": projector_inputs, "assigned_specialist": assigned_specialist, "score_multiplier": score_multiplier, "score_shift": score_shift}


def couple_contributions(picture_batch, caption_batch, score_scaling, neighbour_shift, match_signs):
    pair_scores = score_scaling * lax.dot_general(picture_batch, caption_batch, (((1,), (1,)), ((), ())), preferred_element_type=jnp.float32) + neighbour_shift
    couple_penalty = jnp.sum(jax.nn.softplus(-match_signs * pair_scores), axis=1)
    specialist_projector = (-score_scaling * match_signs * jax.nn.sigmoid(-match_signs * pair_scores)).astype(jnp.bfloat16)
    return couple_penalty, specialist_projector


def reference(picture_vectors, caption_vectors, projector_inputs, assigned_specialist, score_multiplier, score_shift):
    blocks = N_DP * N_EXPERT
    image_block_list = picture_vectors.reshape(blocks, IMG_DEV, E)
    text_blocks = caption_vectors.reshape(blocks, TXT_DEV, E)
    score_scaling = score_multiplier[0]
    neighbour_shift = score_shift[0]
    matches = (jnp.arange(IMG_DEV) // 2)[:, None] == jnp.arange(TXT_DEV)[None, :]
    diagonal_labels = jnp.where(matches, 1.0, -1.0).astype(jnp.float32)
    other_labels = jnp.full((IMG_DEV, TXT_DEV), -1.0, jnp.float32)

    def visit(text_grads, block):
        picture_batch = lax.dynamic_index_in_dim(image_block_list, block, 0, keepdims=False)
        total_loss = jnp.zeros((IMG_DEV,), jnp.float32)
        image_grad = jnp.zeros((IMG_DEV, E), jnp.float32)
        for step in range(STEPS):
            source = ((block - step * N_EXPERT) % blocks).astype(jnp.int32)
            caption_batch = lax.dynamic_index_in_dim(text_blocks, source, 0, keepdims=False)
            match_signs = diagonal_labels if step == 0 else other_labels
            couple_penalty, specialist_projector = couple_contributions(picture_batch, caption_batch, score_scaling, neighbour_shift, match_signs)
            total_loss = total_loss + couple_penalty
            image_grad = image_grad + jnp.dot(specialist_projector, caption_batch, preferred_element_type=jnp.float32)
            partial_value = lax.dot_general(specialist_projector, picture_batch, (((0,), (0,)), ((), ())), preferred_element_type=jnp.float32)
            current = lax.dynamic_index_in_dim(text_grads, source, 0, keepdims=False)
            text_grads = lax.dynamic_update_index_in_dim(text_grads, current + partial_value, source, 0)
        return text_grads, (total_loss, image_grad.astype(jnp.bfloat16))

    text_grads, output_values = lax.scan(visit, jnp.zeros((blocks, TXT_DEV, E), jnp.float32), jnp.arange(blocks, dtype=jnp.int32))
    image_loss, image_grad = output_values
    grads = image_grad.reshape(-1, E)
    target = assigned_specialist[:, 0]
    order = jnp.argsort(target, stable=True)
    sorted_ids = target[order]
    sorted_grads = grads[order]
    sorted_feats = projector_inputs[order]

    def tile_sum(accum, tile):
        start = (tile * IMG_DEV).astype(jnp.int32)
        tile_ids = lax.dynamic_slice_in_dim(sorted_ids, start, IMG_DEV, 0)
        tile_grads = lax.dynamic_slice_in_dim(sorted_grads, start, IMG_DEV, 0)
        tile_feats = lax.dynamic_slice_in_dim(sorted_feats, start, IMG_DEV, 0)

        def per_expert(expert, inner):
            masked = jnp.where((tile_ids == expert)[:, None], tile_feats, jnp.zeros_like(tile_feats))
            part = lax.dot_general(tile_grads, masked, (((0,), (0,)), ((), ())), preferred_element_type=jnp.float32)
            current = lax.dynamic_index_in_dim(inner, expert, 0, keepdims=False)
            return lax.dynamic_update_index_in_dim(inner, current + part, expert, 0)

        return lax.fori_loop(tile_ids[0], tile_ids[IMG_DEV - 1] + 1, per_expert, accum), None

    expert_grad, unused = lax.scan(tile_sum, jnp.zeros((EXPERTS, E, DXW), jnp.float32), jnp.arange(blocks, dtype=jnp.int32))
    return image_loss.reshape(-1), text_grads.reshape(-1, E), expert_grad
```

```python
import jax
import jax.numpy as jnp
from jax import lax
from jax.experimental import pallas as pl
from jax.experimental.pallas import tpu as pltpu
from jax.sharding import PartitionSpec as P

MESH = pl.DeviceIdType.MESH
NX, NY, NZ, ZLO = 4, 8, 16, 8
IMG, TXT, EMB, FEAT = 384, 64, 1024, 640
STEPS = 4
SLOT = 64
HALF = EMB // 2
QUART = 128
BF, F32 = jnp.bfloat16, jnp.float32


def dest_of(x, y, z, core):
    x, y, z = lax.rem(x + NX, NX), lax.rem(y + NY, NY), lax.rem(z + NZ, NZ)
    return (((z // ZLO * NX + x) * NY + y) * 2 + core, lax.rem(z, ZLO))


def offset_of(delta, core):
    sign = 1 - 2 * core
    return (
        (0, 0, 0),
        (0, 1, 0),
        (1, 0, 0),
        (0, 0, 1),
        (0, sign, sign),
        (0, 0, -1),
        (-1, 0, 0),
        (0, -1, 0),
    )[delta]


def kernel(
    img_hbm, txt_hbm, feat_hbm, ids_ref, scale_ref, shift_ref,
    loss_ref, tgrad_ref, egrad_ref,
    img, feat, txt, perm, wts, fsend, fr, ft, gsend, gr, tgs, tgr, s1s, s1r, s2s, s2r, fin_s, fin_r,
    in_sem, txt_ss, txt_rs, f_ss, f_rs, ff_ss, ff_rs, g_ss, g_rs, tg_ss, tg_rs, s1_ss, s1_rs,
    s2_ss, s2_rs, fin_ss, fin_rs,
):
    dp, ex = lax.axis_index("dp"), lax.axis_index("expert")
    n_dp = 2 * NX * NY * (NZ // ZLO)
    core = lax.rem(dp, 2)
    y = lax.rem(dp // 2, NY)
    x = lax.rem(dp // (2 * NY), NX)
    zh = dp // (2 * NY * NX)
    z = zh * ZLO + ex
    other = 1 - core
    sign = 1 - 2 * core
    residue = lax.rem(2 * x + y + 3 * z, 8)
    sibling = (dp + 1 - 2 * core, ex)

    def along(steps):
        return (lax.rem(dp + steps + n_dp, n_dp), ex)

    def remote(src, dst, ss, rs, dev):
        return pltpu.make_async_remote_copy(
            src_ref=src, dst_ref=dst, send_sem=ss, recv_sem=rs, device_id=dev, device_id_type=MESH
        )

    c_img = pltpu.make_async_copy(img_hbm, img, in_sem.at[0])
    c_feat = pltpu.make_async_copy(feat_hbm, feat, in_sem.at[1])
    c_txt = pltpu.make_async_copy(txt_hbm, txt.at[pl.ds(0, TXT)], in_sem.at[2])
    c_feat.start()
    c_txt.start()
    c_img.start()

    barrier = pltpu.get_barrier_semaphore()

    def greet(dev):
        pl.semaphore_signal(barrier, inc=1, device_id=dev, device_id_type=MESH)

    for s in range(1, STEPS):
        greet(along(-s))
        greet(along(s))
    greet(sibling)
    for delta in range(1, 8):
        for cs in range(2):
            dx, dy, dz = offset_of(delta, cs)
            greet(dest_of(x - dx, y - dy, z - dz, cs))
    greet(dest_of(x - 1, y - 1, z + 1, core))
    greet(dest_of(x + 1, y + 1, z - 1, core))
    greet(dest_of(x - 2 * sign, y - 2 * sign, z + 2 * sign, core))

    def source_y(zs):
        return lax.rem(ex + 64 - 2 * x - 3 * zs, 8)

    @pl.when(core == zh)
    def _():
        for zs in range(NZ):
            ys = source_y(zs)

            @pl.when(jnp.logical_or(ys != y, zs != z))
            def _():
                greet(dest_of(x, ys, zs, core))

    to_self = jnp.logical_and(core == zh, residue == ex)
    pl.semaphore_wait(barrier, 6 + 1 + 14 + 3 + 8 - to_self.astype(jnp.int32))

    def txt_copy(s):
        return remote(txt_hbm, txt.at[pl.ds(s * TXT, TXT)], txt_ss.at[s - 1], txt_rs.at[s - 1], along(s))

    for s in range(1, STEPS):
        txt_copy(s).start()

    rel = lax.rem(ids_ref[...] + 8 - residue, 8)
    hot = (rel == lax.broadcasted_iota(jnp.int32, (8, IMG), 0)).astype(BF)
    before = (
        lax.broadcasted_iota(jnp.int32, (IMG, IMG), 0) < lax.broadcasted_iota(jnp.int32, (IMG, IMG), 1)
    ).astype(BF)
    counts = jnp.dot(hot, before, preferred_element_type=F32)
    rank = jnp.sum(counts * hot.astype(F32), axis=0, keepdims=True)
    place = rel * SLOT + rank.astype(jnp.int32)
    perm[...] = jnp.where(
        lax.broadcasted_iota(jnp.int32, (8 * SLOT, IMG), 0) == place, 1.0, 0.0
    ).astype(BF)
    c_feat.wait()
    fsend[...] = jnp.dot(perm[...], feat[...], preferred_element_type=F32).astype(BF)

    def f_copy(delta):
        dx, dy, dz = offset_of(delta, core)
        row = pl.multiple_of((core * 8 + delta) * SLOT, SLOT)
        return remote(
            fsend.at[pl.ds(delta * SLOT, SLOT)], fr.at[pl.ds(row, SLOT)],
            f_ss.at[delta], f_rs.at[delta], dest_of(x + dx, y + dy, z + dz, core),
        )

    for delta in (4, 3, 5, 2, 6, 1, 7):
        f_copy(delta).start()
    own0 = pl.multiple_of(core * 8 * SLOT, SLOT)
    fr[pl.ds(own0, SLOT), :] = fsend[0:SLOT, :]

    scale, shift = scale_ref[0], shift_ref[0]
    c_img.wait()
    c_txt.wait()

    def pairs(first, rows, match):
        block = txt[pl.ds(first, rows), :]
        logits = scale * lax.dot_general(
            block, img[...], (((1,), (1,)), ((), ())), preferred_element_type=F32
        ) + shift
        if match:
            hit = lax.broadcasted_iota(jnp.int32, (rows, IMG), 0) == (
                lax.broadcasted_iota(jnp.int32, (rows, IMG), 1) // 2
            )
            labels = jnp.where(hit, 1.0, -1.0)
            arg = -labels * logits
            amount = -scale * labels
        else:
            arg = logits
            amount = scale
        small = jnp.exp(-jnp.abs(arg))
        loss = jnp.maximum(arg, 0.0) + jnp.log1p(small)
        inv = 1.0 / (1.0 + small)
        sig = jnp.where(arg >= 0.0, inv, small * inv)
        wts[pl.ds(first, rows), :] = (amount * sig).astype(BF)
        return jnp.sum(loss, axis=0, keepdims=True)

    loss = pairs(0, TXT, True)

    for delta in (1, 7, 2, 6, 3, 5, 4):
        f_copy(delta).wait_recv()
    half_rows = pl.ds(own0, 8 * SLOT)
    ff = remote(fr.at[half_rows], fr.at[half_rows], ff_ss, ff_rs, sibling)
    ff.start()

    for s in range(1, STEPS):
        txt_copy(s).wait_recv()
    loss_ref[...] = loss + pairs(TXT, (STEPS - 1) * TXT, False)

    picked = lax.dot_general(
        perm[...], wts[...], (((1,), (1,)), ((), ())), preferred_element_type=F32
    ).astype(BF)
    gsend[...] = jnp.dot(picked, txt[...], preferred_element_type=F32).astype(BF)

    def g_copy(delta, half):
        dx, dy, dz = offset_of(delta, core)
        row = pl.multiple_of((core * 8 + delta) * SLOT, SLOT)
        dev = sibling if delta == 0 else dest_of(x + dx, y + dy, z + dz, half)
        col = half * HALF
        if delta == 0:
            col = pl.multiple_of(other * HALF, HALF)
        return remote(
            gsend.at[pl.ds(delta * SLOT, SLOT), pl.ds(col, HALF)], gr.at[pl.ds(row, SLOT)],
            g_ss.at[delta, half], g_rs.at[core, delta], dev,
        )

    g_list = [(delta, half) for delta in (4, 3, 5, 2, 6, 1, 7) for half in range(2)] + [(0, 0)]
    for delta, half in g_list:
        g_copy(delta, half).start()
    gr[pl.ds(own0, SLOT), :] = gsend[0:SLOT, pl.ds(pl.multiple_of(core * HALF, HALF), HALF)]

    sums = jnp.dot(wts[TXT:, :], img[...], preferred_element_type=F32)
    tgs[...] = sums.astype(BF)

    def tg_copy(s):
        rows = pl.ds((s - 1) * TXT, TXT)
        return remote(tgs.at[rows], tgr.at[rows], tg_ss.at[s - 1], tg_rs.at[s - 1], along(-s))

    for s in range(1, STEPS):
        tg_copy(s).start()
    tgrad_ref[...] = jnp.dot(wts[0:TXT, :], img[...], preferred_element_type=F32)

    ff_in = remote(
        fr.at[pl.ds(pl.multiple_of(other * 8 * SLOT, SLOT), 8 * SLOT)],
        fr.at[pl.ds(pl.multiple_of(other * 8 * SLOT, SLOT), 8 * SLOT)],
        ff_ss, ff_rs, sibling,
    )
    ff_in.wait_recv()
    ft[...] = jnp.transpose(fr[...])

    def g_arrival(cs, delta):
        rows = pl.ds((cs * 8 + delta) * SLOT, SLOT)
        return remote(gr.at[rows], gr.at[rows], g_ss.at[0, 1], g_rs.at[cs, delta], sibling)

    for delta in (1, 7, 2, 6, 3, 5, 4):
        for cs in range(2):
            g_arrival(cs, delta).wait_recv()
    remote(gr.at[pl.ds(0, SLOT)], gr.at[pl.ds(0, SLOT)], g_ss.at[0, 1], g_rs.at[other, 0], sibling).wait_recv()

    def quarter(q):
        col = pl.multiple_of(lax.rem(q + NX, NX) * QUART, QUART)
        return jnp.dot(ft[...], gr[:, pl.ds(col, QUART)], preferred_element_type=F32)

    def s1_copy(i):
        step = (2 * sign, 1, -1)[i]
        return remote(
            s1s.at[i], s1r.at[i], s1_ss.at[i], s1_rs.at[i], dest_of(x + step, y + step, z - step, core)
        )

    for i, q in enumerate((x + 2, x + 1, x - 1)):
        s1s[i] = quarter(q).astype(BF)
        s1_copy(i).start()
    mine = quarter(x)
    for i in (1, 2, 0):
        s1_copy(i).wait_recv()
        mine = mine + s1r[i].astype(F32)
    s2s[...] = jnp.transpose(mine).astype(BF)

    target_z = residue + 8 * core

    def s2_copy(yt):
        row = pl.multiple_of(z * 16, 16)
        return remote(
            s2s.at[pl.ds(yt * 16, 16)], s2r.at[pl.ds(row, 16)], s2_ss.at[yt], s2_rs.at[z],
            dest_of(x, yt, target_z, core),
        )

    for yt in range(NY):
        here = jnp.logical_and(to_self, y == yt)

        @pl.when(jnp.logical_not(here))
        def _():
            s2_copy(yt).start()

        @pl.when(here)
        def _():
            s2r[pl.ds(pl.multiple_of(z * 16, 16), 16), :] = s2s[yt * 16 : yt * 16 + 16, :]

    for s in range(1, STEPS):
        tg_copy(s).wait_recv()
    tgrad_ref[...] += (
        tgr[0:TXT, :].astype(F32) + tgr[TXT : 2 * TXT, :].astype(F32) + tgr[2 * TXT :, :].astype(F32)
    )

    fin = remote(
        fin_s.at[pl.ds(pl.multiple_of(other * 8, 8), 8)], fin_r, fin_ss, fin_rs, sibling
    )

    @pl.when(core == zh)
    def _():
        for zs in range(NZ):

            @pl.when(jnp.logical_or(source_y(zs) != y, zs != z))
            def _():
                rows = pl.ds(zs * 16, 16)
                remote(s2r.at[rows], s2r.at[rows], s2_ss.at[0], s2_rs.at[zs], sibling).wait_recv()

        total = s2r[0:16, :].astype(F32)
        for zs in range(1, NZ):
            total = total + s2r[zs * 16 : zs * 16 + 16, :].astype(F32)
        fin_s[...] = total
        fin.start()
        egrad_ref[0] = fin_s[pl.ds(pl.multiple_of(core * 8, 8), 8), :]
        fin.wait_send()

    @pl.when(core != zh)
    def _():
        fin.wait_recv()
        egrad_ref[0] = fin_r[...]

    for s in range(1, STEPS):
        txt_copy(s).wait_send()
        tg_copy(s).wait_send()
    for delta in range(1, 8):
        f_copy(delta).wait_send()
    ff.wait_send()
    for delta, half in g_list:
        g_copy(delta, half).wait_send()
    for i in range(3):
        s1_copy(i).wait_send()
    for yt in range(NY):

        @pl.when(jnp.logical_not(jnp.logical_and(to_self, y == yt)))
        def _():
            s2_copy(yt).wait_send()


def on_device(images, texts, feats, ids, scale, shift):
    vmem, smem, dma = pltpu.VMEM, pltpu.SMEM, pltpu.SemaphoreType.DMA
    loss, tgrad, egrad = pl.pallas_call(
        kernel,
        out_shape=(
            jax.ShapeDtypeStruct((1, IMG), F32),
            jax.ShapeDtypeStruct((TXT, EMB), F32),
            jax.ShapeDtypeStruct((1, 8, FEAT), F32),
        ),
        in_specs=[
            pl.BlockSpec(memory_space=pl.ANY),
            pl.BlockSpec(memory_space=pl.ANY),
            pl.BlockSpec(memory_space=pl.ANY),
            pl.BlockSpec(memory_space=vmem),
            pl.BlockSpec(memory_space=smem),
            pl.BlockSpec(memory_space=smem),
        ],
        out_specs=(
            pl.BlockSpec(memory_space=vmem),
            pl.BlockSpec(memory_space=vmem),
            pl.BlockSpec(memory_space=vmem),
        ),
        scratch_shapes=[
            vmem((IMG, EMB), BF),
            vmem((IMG, FEAT), BF),
            vmem((STEPS * TXT, EMB), BF),
            vmem((8 * SLOT, IMG), BF),
            vmem((STEPS * TXT, IMG), BF),
            vmem((8 * SLOT, FEAT), BF),
            vmem((16 * SLOT, FEAT), BF),
            vmem((FEAT, 16 * SLOT), BF),
            vmem((8 * SLOT, EMB), BF),
            vmem((16 * SLOT, HALF), BF),
            vmem(((STEPS - 1) * TXT, EMB), BF),
            vmem(((STEPS - 1) * TXT, EMB), BF),
            vmem((3, FEAT, QUART), BF),
            vmem((3, FEAT, QUART), BF),
            vmem((QUART, FEAT), BF),
            vmem((NZ * 16, FEAT), BF),
            vmem((16, FEAT), F32),
            vmem((8, FEAT), F32),
            dma((3,)),
            dma((STEPS - 1,)),
            dma((STEPS - 1,)),
            dma((8,)),
            dma((8,)),
            dma,
            dma,
            dma((8, 2)),
            dma((2, 8)),
            dma((STEPS - 1,)),
            dma((STEPS - 1,)),
            dma((3,)),
            dma((3,)),
            dma((NY,)),
            dma((NZ,)),
            dma,
            dma,
        ],
        compiler_params=pltpu.CompilerParams(
            collective_id=0, has_side_effects=True, vmem_limit_bytes=48 * 1024 * 1024
        ),
        cost_estimate=pl.CostEstimate(flops=2_000_000_000, bytes_accessed=8_000_000, transcendentals=300_000),
    )(images, texts, feats, ids.reshape(1, IMG), scale, shift)
    return loss.reshape(IMG), tgrad, egrad


def solution(mesh):
    both = P(("dp", "expert"), None)
    return jax.shard_map(
        on_device,
        mesh=mesh,
        in_specs=(both, both, both, both, P(), P()),
        out_specs=(P(("dp", "expert")), both, P("expert", "dp", None)),
        check_vma=False,
    )
```

```python
import jax
import jax.numpy as jnp
from jax import lax
from jax.experimental import pallas as pl
from jax.experimental.pallas import tpu as pltpu
from jax.sharding import PartitionSpec as P

MESH = pl.DeviceIdType.MESH
NX, NY, NZ, ZLO = 4, 8, 16, 8
IMG, TXT, EMB, FEAT = 384, 64, 1024, 640
STEPS = 4
SLOT = 64
RUN = 64
PIECE = 128
HALF = EMB // 2
QUART = 128
BF, F32 = jnp.bfloat16, jnp.float32


def dest_of(x, y, z, core):
    x, y, z = lax.rem(x + NX, NX), lax.rem(y + NY, NY), lax.rem(z + NZ, NZ)
    return (((z // ZLO * NX + x) * NY + y) * 2 + core, lax.rem(z, ZLO))


def offset_of(delta, core):
    sign = 1 - 2 * core
    return (
        (0, 0, 0),
        (0, 1, 0),
        (1, 0, 0),
        (0, 0, 1),
        (0, sign, sign),
        (0, 0, -1),
        (-1, 0, 0),
        (0, -1, 0),
    )[delta]


def kernel(
    img_hbm, txt_hbm, feat_hbm, ids_ref, scale_ref, shift_ref,
    loss_ref, tgrad_ref, egrad_ref,
    img, feat, txt, perm, wts, fsend, fr, ft, gsend, gr, tgs, tgr, s1s, s1r, s2s, s2r, fin_s, fin_r,
    hop_a, hop_b, back_a, back_b,
    in_sem, txt_ss, txt_rs, f_ss, f_rs, ff_ss, ff_rs, g_ss, g_rs, tg_ss, tg_rs, s1_ss, s1_rs,
    s2_ss, s2_rs, fin_ss, fin_rs,
    rel_ss, hop_as, hop_ar, hop_bs, hop_br, hop_cs, back_ar, back_bs, back_br, back_cs,
):
    dp, ex = lax.axis_index("dp"), lax.axis_index("expert")
    n_dp = 2 * NX * NY * (NZ // ZLO)
    core = lax.rem(dp, 2)
    y = lax.rem(dp // 2, NY)
    x = lax.rem(dp // (2 * NY), NX)
    zh = dp // (2 * NY * NX)
    z = zh * ZLO + ex
    other = 1 - core
    sign = 1 - 2 * core
    residue = lax.rem(2 * x + y + 3 * z, 8)
    sibling = (dp + 1 - 2 * core, ex)

    def along(steps):
        return (lax.rem(dp + steps + n_dp, n_dp), ex)

    def remote(src, dst, ss, rs, dev):
        return pltpu.make_async_remote_copy(
            src_ref=src, dst_ref=dst, send_sem=ss, recv_sem=rs, device_id=dev, device_id_type=MESH
        )

    c_img = pltpu.make_async_copy(img_hbm, img, in_sem.at[0])
    c_feat = pltpu.make_async_copy(feat_hbm, feat, in_sem.at[1])
    c_txt = pltpu.make_async_copy(txt_hbm, txt.at[pl.ds(0, TXT)], in_sem.at[2])
    c_feat.start()
    c_txt.start()
    c_img.start()

    barrier = pltpu.get_barrier_semaphore()

    def greet(dev):
        pl.semaphore_signal(barrier, inc=1, device_id=dev, device_id_type=MESH)

    at = lax.rem(dp, RUN)

    def inside(steps):
        return jnp.logical_and(at + steps >= 0, at + steps < RUN)

    for s in range(1, STEPS):
        for steps in (-s, s):

            @pl.when(inside(steps))
            def _():
                greet(along(steps))

    greet(sibling)
    for delta in range(1, 8):
        for cs in range(2):
            dx, dy, dz = offset_of(delta, cs)
            greet(dest_of(x - dx, y - dy, z - dz, cs))
    greet(dest_of(x - 1, y - 1, z + 1, core))
    greet(dest_of(x + 1, y + 1, z - 1, core))
    greet(dest_of(x - 2 * sign, y - 2 * sign, z + 2 * sign, core))

    def source_y(zs):
        return lax.rem(ex + 64 - 2 * x - 3 * zs, 8)

    @pl.when(core == zh)
    def _():
        for zs in range(NZ):
            ys = source_y(zs)

            @pl.when(jnp.logical_or(ys != y, zs != z))
            def _():
                greet(dest_of(x, ys, zs, core))

    lean = 2 * core - 1
    is_relay = jnp.logical_and(jnp.logical_or(x == 1, x == 2), jnp.logical_or(y >= NY - 2, y <= 1))
    piece = lax.rem((x - 1) * 4 + lax.rem(y + 2, NY) + 8, 8)
    piece_cols = pl.ds(pl.multiple_of(piece * PIECE, PIECE), PIECE)
    is_last = [at == RUN - 1 - i for i in range(3)]
    is_first = [at == i for i in range(3)]

    def relay_of(j, plane, c):
        return dest_of(1 + j // 4, (6 + j % 4) % NY, plane, c)

    def last_dev(i, plane):
        return dest_of(NX - 1, NY - 1 - (i + 0) // 2, plane, 1 - i % 2)

    def first_dev(i, plane):
        return dest_of(0, i // 2, plane, i % 2)

    @pl.when(is_relay)
    def _():
        greet(dest_of(x, y, z - ZLO + lean, core))

        @pl.when(core == 1)
        def _():
            greet(last_dev(0, z - lean))
            for i in range(3):
                greet(first_dev(i, z - lean))

        @pl.when(core == 0)
        def _():
            for i in (1, 2):
                greet(last_dev(i, z - lean))
            for i in range(2):
                greet(first_dev(i, z - lean))

    for i in range(3):

        @pl.when(is_last[i])
        def _():
            for j in range(8):
                greet(relay_of(j, z, 1 if i == 0 else 0))

        @pl.when(is_first[i])
        def _():
            for j in range(8):
                greet(relay_of(j, z, 1))
                if i < 2:
                    greet(relay_of(j, z, 0))

    def one(flag):
        return flag.astype(jnp.int32)

    to_self = jnp.logical_and(core == zh, residue == ex)
    outs = 1 + 14 + 3 + 8 - one(to_self) + 5 * one(is_relay)
    for s in range(1, STEPS):
        outs = outs + one(inside(s)) + one(inside(-s))
    for i in range(3):
        outs = outs + 8 * one(is_last[i]) + (16 if i < 2 else 8) * one(is_first[i])
    pl.semaphore_wait(barrier, outs)

    def txt_copy(s):
        return remote(txt_hbm, txt.at[pl.ds(s * TXT, TXT)], txt_ss.at[s - 1], txt_rs.at[s - 1], along(s))

    def rel_copy(i, j):
        c = 1 if i == 0 else 0
        return remote(
            txt_hbm.at[:, pl.ds(j * PIECE, PIECE)], hop_a.at[1 if i == 2 else 0],
            rel_ss, hop_ar.at[1 if i == 2 else 0], relay_of(j, z + 2 * c - 1, c),
        )

    for i in range(3):

        @pl.when(is_last[i])
        def _():
            for j in range(8):
                rel_copy(i, j).start()

    for s in (3, 2, 1):

        @pl.when(inside(s))
        def _():
            txt_copy(s).start()

    def hop_copy(slot):
        return remote(
            hop_a.at[slot], hop_b.at[slot], hop_as.at[slot], hop_br.at[slot],
            dest_of(x, y, z + ZLO - lean, core),
        )

    def hop_arrival(slot):
        return remote(hop_a.at[slot], hop_a.at[slot], hop_as.at[slot], hop_ar.at[slot], sibling)

    @pl.when(is_relay)
    def _():
        hop_arrival(0).wait_recv()
        hop_copy(0).start()

        @pl.when(core == 0)
        def _():
            hop_arrival(1).wait_recv()
            hop_copy(1).start()

    fan1 = ((0, 0, 1), (0, 1, 2), (0, 2, 3))
    fan0 = ((0, 0, 2), (0, 1, 3), (1, 0, 3))

    def fan_copy(n, slot, i, s):
        return remote(
            hop_b.at[slot], txt.at[pl.ds(s * TXT, TXT), piece_cols], hop_cs.at[n], txt_rs.at[s - 1], first_dev(i, z)
        )

    rel = lax.rem(ids_ref[...] + 8 - residue, 8)
    hot = (rel == lax.broadcasted_iota(jnp.int32, (8, IMG), 0)).astype(BF)
    before = (
        lax.broadcasted_iota(jnp.int32, (IMG, IMG), 0) < lax.broadcasted_iota(jnp.int32, (IMG, IMG), 1)
    ).astype(BF)
    counts = jnp.dot(hot, before, preferred_element_type=F32)
    rank = jnp.sum(counts * hot.astype(F32), axis=0, keepdims=True)
    place = rel * SLOT + rank.astype(jnp.int32)
    perm[...] = jnp.where(
        lax.broadcasted_iota(jnp.int32, (8 * SLOT, IMG), 0) == place, 1.0, 0.0
    ).astype(BF)
    c_feat.wait()
    fsend[...] = jnp.dot(perm[...], feat[...], preferred_element_type=F32).astype(BF)

    def f_copy(delta):
        dx, dy, dz = offset_of(delta, core)
        row = pl.multiple_of((core * 8 + delta) * SLOT, SLOT)
        return remote(
            fsend.at[pl.ds(delta * SLOT, SLOT)], fr.at[pl.ds(row, SLOT)],
            f_ss.at[delta], f_rs.at[delta], dest_of(x + dx, y + dy, z + dz, core),
        )

    for delta in (4, 3, 5, 2, 6, 1, 7):
        f_copy(delta).start()
    @pl.when(is_relay)
    def _():
        for c, fan in ((1, fan1), (0, fan0)):

            @pl.when(core == c)
            def _():
                for slot in range(2 - c):
                    hop_copy(slot).wait_recv()
                    for n in range(3):
                        if fan[n][0] == slot:
                            fan_copy(n, *fan[n]).start()

    own0 = pl.multiple_of(core * 8 * SLOT, SLOT)
    fr[pl.ds(own0, SLOT), :] = fsend[0:SLOT, :]

    scale, shift = scale_ref[0], shift_ref[0]
    c_img.wait()
    c_txt.wait()

    def pairs(first, rows, match):
        block = txt[pl.ds(first, rows), :]
        logits = scale * lax.dot_general(
            block, img[...], (((1,), (1,)), ((), ())), preferred_element_type=F32
        ) + shift
        if match:
            hit = lax.broadcasted_iota(jnp.int32, (rows, IMG), 0) == (
                lax.broadcasted_iota(jnp.int32, (rows, IMG), 1) // 2
            )
            labels = jnp.where(hit, 1.0, -1.0)
            arg = -labels * logits
            amount = -scale * labels
        else:
            arg = logits
            amount = scale
        small = jnp.exp(-jnp.abs(arg))
        loss = jnp.maximum(arg, 0.0) + jnp.log1p(small)
        inv = 1.0 / (1.0 + small)
        sig = jnp.where(arg >= 0.0, inv, small * inv)
        wts[pl.ds(first, rows), :] = (amount * sig).astype(BF)
        return jnp.sum(loss, axis=0, keepdims=True)

    loss = pairs(0, TXT, True)

    for delta in (1, 7, 2, 6, 3, 5, 4):
        f_copy(delta).wait_recv()
    half_rows = pl.ds(own0, 8 * SLOT)
    ff = remote(fr.at[half_rows], fr.at[half_rows], ff_ss, ff_rs, sibling)
    ff.start()

    for s in range(1, STEPS):
        txt_copy(s).wait_recv()
    loss_ref[...] = loss + pairs(TXT, (STEPS - 1) * TXT, False)

    picked = lax.dot_general(
        perm[...], wts[...], (((1,), (1,)), ((), ())), preferred_element_type=F32
    ).astype(BF)
    gsend[...] = jnp.dot(picked, txt[...], preferred_element_type=F32).astype(BF)

    def g_copy(delta, half):
        dx, dy, dz = offset_of(delta, core)
        row = pl.multiple_of((core * 8 + delta) * SLOT, SLOT)
        dev = sibling if delta == 0 else dest_of(x + dx, y + dy, z + dz, half)
        col = half * HALF
        if delta == 0:
            col = pl.multiple_of(other * HALF, HALF)
        return remote(
            gsend.at[pl.ds(delta * SLOT, SLOT), pl.ds(col, HALF)], gr.at[pl.ds(row, SLOT)],
            g_ss.at[delta, half], g_rs.at[core, delta], dev,
        )

    g_list = [(delta, half) for delta in (4, 3, 5, 2, 6, 1, 7) for half in range(2)] + [(0, 0)]
    for delta, half in g_list:
        g_copy(delta, half).start()
    gr[pl.ds(own0, SLOT), :] = gsend[0:SLOT, pl.ds(pl.multiple_of(core * HALF, HALF), HALF)]

    sums = jnp.dot(wts[TXT:, :], img[...], preferred_element_type=F32)
    tgs[...] = sums.astype(BF)

    def tg_copy(s):
        rows = pl.ds((s - 1) * TXT, TXT)
        return remote(tgs.at[rows], tgr.at[rows], tg_ss.at[s - 1], tg_rs.at[s - 1], along(-s))

    back = ((0, 1, 0, 1), (0, 2, 0, 0), (0, 3, 2, 0), (1, 2, 1, 1), (1, 3, 1, 0), (2, 3, 2, 1))

    def back_out(s, slot, c, j):
        return remote(
            tgs.at[pl.ds((s - 1) * TXT, TXT), pl.ds(j * PIECE, PIECE)], back_a.at[slot],
            tg_ss.at[s - 1], back_ar.at[slot], relay_of(j, z + 2 * c - 1, c),
        )

    for i, s, slot, c in back:

        @pl.when(is_first[i])
        def _():
            for j in range(8):
                back_out(s, slot, c, j).start()

    for s in range(1, STEPS):

        @pl.when(inside(-s))
        def _():
            tg_copy(s).start()

    tgrad_ref[...] = jnp.dot(wts[0:TXT, :], img[...], preferred_element_type=F32)

    ff_in = remote(
        fr.at[pl.ds(pl.multiple_of(other * 8 * SLOT, SLOT), 8 * SLOT)],
        fr.at[pl.ds(pl.multiple_of(other * 8 * SLOT, SLOT), 8 * SLOT)],
        ff_ss, ff_rs, sibling,
    )
    ff_in.wait_recv()
    ft[...] = jnp.transpose(fr[...])

    def g_arrival(cs, delta):
        rows = pl.ds((cs * 8 + delta) * SLOT, SLOT)
        return remote(gr.at[rows], gr.at[rows], g_ss.at[0, 1], g_rs.at[cs, delta], sibling)

    for delta in (1, 7, 2, 6, 3, 5, 4):
        for cs in range(2):
            g_arrival(cs, delta).wait_recv()
    remote(gr.at[pl.ds(0, SLOT)], gr.at[pl.ds(0, SLOT)], g_ss.at[0, 1], g_rs.at[other, 0], sibling).wait_recv()

    def quarter(q):
        col = pl.multiple_of(lax.rem(q + NX, NX) * QUART, QUART)
        return jnp.dot(ft[...], gr[:, pl.ds(col, QUART)], preferred_element_type=F32)

    def s1_copy(i):
        step = (2 * sign, 1, -1)[i]
        return remote(
            s1s.at[i], s1r.at[i], s1_ss.at[i], s1_rs.at[i], dest_of(x + step, y + step, z - step, core)
        )

    for i, q in enumerate((x + 2, x + 1, x - 1)):
        s1s[i] = quarter(q).astype(BF)
        s1_copy(i).start()
    back_copy = remote(back_a, back_b, back_bs, back_br, dest_of(x, y, z + ZLO - lean, core))

    @pl.when(is_relay)
    def _():
        for slot in range(3):
            remote(back_a.at[slot], back_a.at[slot], back_bs, back_ar.at[slot], sibling).wait_recv()
        back_copy.start()

    mine = quarter(x)
    for i in (1, 2, 0):
        s1_copy(i).wait_recv()
        mine = mine + s1r[i].astype(F32)
    s2s[...] = jnp.transpose(mine).astype(BF)

    target_z = residue + 8 * core

    def s2_copy(yt):
        row = pl.multiple_of(z * 16, 16)
        return remote(
            s2s.at[pl.ds(yt * 16, 16)], s2r.at[pl.ds(row, 16)], s2_ss.at[yt], s2_rs.at[z],
            dest_of(x, yt, target_z, core),
        )

    for yt in range(NY):
        here = jnp.logical_and(to_self, y == yt)

        @pl.when(jnp.logical_not(here))
        def _():
            s2_copy(yt).start()

        @pl.when(here)
        def _():
            s2r[pl.ds(pl.multiple_of(z * 16, 16), 16), :] = s2s[yt * 16 : yt * 16 + 16, :]

    home1 = ((0, 0, 1), (1, 0, 2), (2, 0, 3))
    home0 = ((0, 1, 2), (1, 1, 3), (2, 2, 3))

    def home_copy(slot, i, s):
        return remote(
            back_b.at[slot], tgr.at[pl.ds((s - 1) * TXT, TXT), piece_cols],
            back_cs.at[slot], tg_rs.at[s - 1], last_dev(i, z),
        )

    @pl.when(is_relay)
    def _():
        back_copy.wait_recv()
        for c, home in ((1, home1), (0, home0)):

            @pl.when(core == c)
            def _():
                for args in home:
                    home_copy(*args).start()

    for s in range(1, STEPS):
        tg_copy(s).wait_recv()
    tgrad_ref[...] += (
        tgr[0:TXT, :].astype(F32) + tgr[TXT : 2 * TXT, :].astype(F32) + tgr[2 * TXT :, :].astype(F32)
    )

    fin = remote(
        fin_s.at[pl.ds(pl.multiple_of(other * 8, 8), 8)], fin_r, fin_ss, fin_rs, sibling
    )

    @pl.when(core == zh)
    def _():
        for zs in range(NZ):

            @pl.when(jnp.logical_or(source_y(zs) != y, zs != z))
            def _():
                rows = pl.ds(zs * 16, 16)
                remote(s2r.at[rows], s2r.at[rows], s2_ss.at[0], s2_rs.at[zs], sibling).wait_recv()

        total = s2r[0:16, :].astype(F32)
        for zs in range(1, NZ):
            total = total + s2r[zs * 16 : zs * 16 + 16, :].astype(F32)
        fin_s[...] = total
        fin.start()
        egrad_ref[0] = fin_s[pl.ds(pl.multiple_of(core * 8, 8), 8), :]
        fin.wait_send()

    @pl.when(core != zh)
    def _():
        fin.wait_recv()
        egrad_ref[0] = fin_r[...]

    for s in range(1, STEPS):

        @pl.when(inside(s))
        def _():
            txt_copy(s).wait_send()

        tg_copy(s).wait_send()

    @pl.when(at >= RUN - 3)
    def _():
        remote(txt_hbm, txt.at[pl.ds(0, TXT)], rel_ss, txt_rs.at[0], sibling).wait_send()

    @pl.when(is_relay)
    def _():
        hop_copy(0).wait_send()

        @pl.when(core == 0)
        def _():
            hop_copy(1).wait_send()

        for n in range(3):
            fan_copy(n, *fan1[0]).wait_send()
            home_copy(*home1[n]).wait_send()
        back_copy.wait_send()

    for delta in range(1, 8):
        f_copy(delta).wait_send()
    ff.wait_send()
    for delta, half in g_list:
        g_copy(delta, half).wait_send()
    for i in range(3):
        s1_copy(i).wait_send()
    for yt in range(NY):

        @pl.when(jnp.logical_not(jnp.logical_and(to_self, y == yt)))
        def _():
            s2_copy(yt).wait_send()


def on_device(images, texts, feats, ids, scale, shift):
    vmem, smem, dma = pltpu.VMEM, pltpu.SMEM, pltpu.SemaphoreType.DMA
    loss, tgrad, egrad = pl.pallas_call(
        kernel,
        out_shape=(
            jax.ShapeDtypeStruct((1, IMG), F32),
            jax.ShapeDtypeStruct((TXT, EMB), F32),
            jax.ShapeDtypeStruct((1, 8, FEAT), F32),
        ),
        in_specs=[
            pl.BlockSpec(memory_space=pl.ANY),
            pl.BlockSpec(memory_space=pl.ANY),
            pl.BlockSpec(memory_space=pl.ANY),
            pl.BlockSpec(memory_space=vmem),
            pl.BlockSpec(memory_space=smem),
            pl.BlockSpec(memory_space=smem),
        ],
        out_specs=(
            pl.BlockSpec(memory_space=vmem),
            pl.BlockSpec(memory_space=vmem),
            pl.BlockSpec(memory_space=vmem),
        ),
        scratch_shapes=[
            vmem((IMG, EMB), BF),
            vmem((IMG, FEAT), BF),
            vmem((STEPS * TXT, EMB), BF),
            vmem((8 * SLOT, IMG), BF),
            vmem((STEPS * TXT, IMG), BF),
            vmem((8 * SLOT, FEAT), BF),
            vmem((16 * SLOT, FEAT), BF),
            vmem((FEAT, 16 * SLOT), BF),
            vmem((8 * SLOT, EMB), BF),
            vmem((16 * SLOT, HALF), BF),
            vmem(((STEPS - 1) * TXT, EMB), BF),
            vmem(((STEPS - 1) * TXT, EMB), BF),
            vmem((3, FEAT, QUART), BF),
            vmem((3, FEAT, QUART), BF),
            vmem((QUART, FEAT), BF),
            vmem((NZ * 16, FEAT), BF),
            vmem((16, FEAT), F32),
            vmem((8, FEAT), F32),
            vmem((2, TXT, PIECE), BF),
            vmem((2, TXT, PIECE), BF),
            vmem((3, TXT, PIECE), BF),
            vmem((3, TXT, PIECE), BF),
            dma((3,)),
            dma((STEPS - 1,)),
            dma((STEPS - 1,)),
            dma((8,)),
            dma((8,)),
            dma,
            dma,
            dma((8, 2)),
            dma((2, 8)),
            dma((STEPS - 1,)),
            dma((STEPS - 1,)),
            dma((3,)),
            dma((3,)),
            dma((NY,)),
            dma((NZ,)),
            dma,
            dma,
            dma,
            dma((2,)),
            dma((2,)),
            dma((2,)),
            dma((2,)),
            dma((3,)),
            dma((3,)),
            dma,
            dma,
            dma((3,)),
        ],
        compiler_params=pltpu.CompilerParams(
            collective_id=0, has_side_effects=True, vmem_limit_bytes=48 * 1024 * 1024
        ),
        cost_estimate=pl.CostEstimate(flops=2_000_000_000, bytes_accessed=8_000_000, transcendentals=300_000),
    )(images, texts, feats, ids.reshape(1, IMG), scale, shift)
    return loss.reshape(IMG), tgrad, egrad


def solution(mesh):
    both = P(("dp", "expert"), None)
    return jax.shard_map(
        on_device,
        mesh=mesh,
        in_specs=(both, both, both, both, P(), P()),
        out_specs=(P(("dp", "expert")), both, P("expert", "dp", None)),
        check_vma=False,
    )
```

```python
import jax
import jax.numpy as jnp
from jax import lax
from jax.experimental import pallas as pl
from jax.experimental.pallas import tpu as pltpu
from jax.sharding import PartitionSpec as P

MESH = pl.DeviceIdType.MESH
NX, NY, NZ, ZLO = 4, 8, 16, 8
IMG, TXT, EMB, FEAT = 384, 64, 1024, 640
STEPS = 4
SLOT = 64
RUN = 64
PIECE = 128
VLIM = (64 * 1024 - 320) * 1024
HALF = EMB // 2
QUART = 128
CHUNKS = ((0, 384), (384, 640))
BF, F32 = jnp.bfloat16, jnp.float32


def dest_of(x, y, z, core):
    x, y, z = lax.rem(x + NX, NX), lax.rem(y + NY, NY), lax.rem(z + NZ, NZ)
    return (((z // ZLO * NX + x) * NY + y) * 2 + core, lax.rem(z, ZLO))


def offset_of(delta, core):
    sign = 1 - 2 * core
    return (
        (0, 0, 0),
        (0, 1, 0),
        (1, 0, 0),
        (0, 0, 1),
        (0, sign, sign),
        (0, 0, -1),
        (-1, 0, 0),
        (0, -1, 0),
    )[delta]


def kernel(
    img_hbm, txt_hbm, feat_hbm, ids_ref, scale_ref, shift_ref,
    loss_ref, tgrad_ref, egrad_ref,
    img, feat, txt, perm, wts, fsend, fr, ft, gsend, gr, tgs, tgr, s1s, s1r, s2s, s2r, fin_s, fin_r,
    hop_a, hop_b, back_a, back_b,
    in_sem, txt_ss, txt_rs, f_ss, f_rs, ff_ss, ff_rs, g_ss, g_rs, tg_ss, tg_rs, s1_ss, s1_rs,
    s2_ss, s2_rs, fin_ss, fin_rs,
    hand_ss, rel_ss, hop_as, hop_ar, hop_bs, hop_br, hop_cs, back_ar, back_bs, back_br, back_cs,
):
    dp, ex = lax.axis_index("dp"), lax.axis_index("expert")
    n_dp = 2 * NX * NY * (NZ // ZLO)
    core = lax.rem(dp, 2)
    y = lax.rem(dp // 2, NY)
    x = lax.rem(dp // (2 * NY), NX)
    zh = dp // (2 * NY * NX)
    z = zh * ZLO + ex
    other = 1 - core
    sign = 1 - 2 * core
    residue = lax.rem(2 * x + y + 3 * z, 8)
    sibling = (dp + 1 - 2 * core, ex)

    def along(steps):
        return (lax.rem(dp + steps + n_dp, n_dp), ex)

    def remote(src, dst, ss, rs, dev):
        return pltpu.make_async_remote_copy(
            src_ref=src, dst_ref=dst, send_sem=ss, recv_sem=rs, device_id=dev, device_id_type=MESH
        )

    c_img = pltpu.make_async_copy(img_hbm, img, in_sem.at[0])
    c_feat = pltpu.make_async_copy(feat_hbm, feat, in_sem.at[1])
    c_txt = pltpu.make_async_copy(txt_hbm, txt.at[pl.ds(0, TXT)], in_sem.at[2])
    c_feat.start()
    c_txt.start()
    c_img.start()

    barrier = pltpu.get_barrier_semaphore()

    def greet(dev):
        pl.semaphore_signal(barrier, inc=1, device_id=dev, device_id_type=MESH)

    at = lax.rem(dp, RUN)

    def inside(steps):
        return jnp.logical_and(at + steps >= 0, at + steps < RUN)

    for s in range(1, STEPS):
        for steps in (-s, s):

            @pl.when(inside(steps))
            def _():
                greet(along(steps))

    greet(sibling)
    for delta in range(1, 8):
        for cs in range(2):
            dx, dy, dz = offset_of(delta, cs)
            greet(dest_of(x - dx, y - dy, z - dz, cs))
    greet(dest_of(x - 1, y - 1, z + 1, core))
    greet(dest_of(x + 1, y + 1, z - 1, core))
    greet(dest_of(x - 2 * sign, y - 2 * sign, z + 2 * sign, core))

    def source_y(zs):
        return lax.rem(ex + 64 - 2 * x - 3 * zs, 8)

    @pl.when(core == zh)
    def _():
        for zs in range(NZ):
            ys = source_y(zs)

            @pl.when(jnp.logical_or(ys != y, zs != z))
            def _():
                greet(dest_of(x, ys, zs, core))

    lean = 2 * core - 1
    is_relay = jnp.logical_and(jnp.logical_or(x == 1, x == 2), jnp.logical_or(y >= NY - 2, y <= 1))
    piece = lax.rem((x - 1) * 4 + lax.rem(y + 2, NY) + 8, 8)
    piece_cols = pl.ds(pl.multiple_of(piece * PIECE, PIECE), PIECE)
    is_last = [at == RUN - 1 - i for i in range(3)]
    is_first = [at == i for i in range(3)]

    def relay_of(j, plane, c):
        return dest_of(1 + j // 4, (6 + j % 4) % NY, plane, c)

    def last_dev(i, plane):
        return dest_of(NX - 1, NY - 1 - (i + 0) // 2, plane, 1 - i % 2)

    def first_dev(i, plane):
        return dest_of(0, i // 2, plane, i % 2)

    @pl.when(is_relay)
    def _():
        greet(dest_of(x, y, z - ZLO + lean, core))

        @pl.when(core == 1)
        def _():
            greet(last_dev(0, z - lean))
            for i in range(3):
                greet(first_dev(i, z - lean))

        @pl.when(core == 0)
        def _():
            for i in (1, 2):
                greet(last_dev(i, z - lean))
            for i in range(2):
                greet(first_dev(i, z - lean))

    for i in range(3):

        @pl.when(is_last[i])
        def _():
            for j in range(8):
                greet(relay_of(j, z, 1 if i == 0 else 0))

        @pl.when(is_first[i])
        def _():
            for j in range(8):
                greet(relay_of(j, z, 1))
                if i < 2:
                    greet(relay_of(j, z, 0))

    def one(flag):
        return flag.astype(jnp.int32)

    to_self = jnp.logical_and(core == zh, residue == ex)
    outs = 1 + 14 + 3 + 8 - one(to_self) + 5 * one(is_relay)
    for s in range(1, STEPS):
        outs = outs + one(inside(s)) + one(inside(-s))
    for i in range(3):
        outs = outs + 8 * one(is_last[i]) + (16 if i < 2 else 8) * one(is_first[i])
    pl.semaphore_wait(barrier, outs)

    def txt_copy(s):
        return remote(txt_hbm, txt.at[pl.ds(s * TXT, TXT)], txt_ss.at[s - 1], txt_rs.at[s - 1], along(s))

    def rel_copy(i, j):
        c = 1 if i == 0 else 0
        return remote(
            txt_hbm.at[:, pl.ds(j * PIECE, PIECE)], hop_a.at[1 if i == 2 else 0],
            rel_ss, hop_ar.at[1 if i == 2 else 0], relay_of(j, z + 2 * c - 1, c),
        )

    for i in range(3):

        @pl.when(is_last[i])
        def _():
            for j in range(8):
                rel_copy(i, j).start()

    sends = ((2, inside(2)), (3, jnp.logical_and(core == 1, inside(3))), (1, core == 0))
    for s, flag in sends:

        @pl.when(flag)
        def _():
            txt_copy(s).start()

    hand = 3 - 2 * core
    handed = remote(
        txt.at[pl.ds(2 * TXT, TXT)], txt.at[pl.ds(pl.multiple_of(hand * TXT, TXT), TXT)],
        hand_ss, txt_rs.at[hand - 1], sibling,
    )

    def hop_copy(slot):
        return remote(
            hop_a.at[slot], hop_b.at[slot], hop_as.at[slot], hop_br.at[slot],
            dest_of(x, y, z + ZLO - lean, core),
        )

    def hop_arrival(slot):
        return remote(hop_a.at[slot], hop_a.at[slot], hop_as.at[slot], hop_ar.at[slot], sibling)

    @pl.when(is_relay)
    def _():
        hop_arrival(0).wait_recv()
        hop_copy(0).start()

        @pl.when(core == 0)
        def _():
            hop_arrival(1).wait_recv()
            hop_copy(1).start()

    fan1 = ((0, 0, 1), (0, 1, 2), (0, 2, 3))
    fan0 = ((0, 0, 2), (0, 1, 3), (1, 0, 3))

    def fan_copy(n, slot, i, s):
        return remote(
            hop_b.at[slot], txt.at[pl.ds(s * TXT, TXT), piece_cols], hop_cs.at[n], txt_rs.at[s - 1], first_dev(i, z)
        )

    rel = lax.rem(ids_ref[...] + 8 - residue, 8)
    hot = (rel == lax.broadcasted_iota(jnp.int32, (8, IMG), 0)).astype(BF)
    before = (
        lax.broadcasted_iota(jnp.int32, (IMG, IMG), 0) < lax.broadcasted_iota(jnp.int32, (IMG, IMG), 1)
    ).astype(BF)
    counts = jnp.dot(hot, before, preferred_element_type=F32)
    rank = jnp.sum(counts * hot.astype(F32), axis=0, keepdims=True)
    place = rel * SLOT + rank.astype(jnp.int32)
    perm[...] = jnp.where(
        lax.broadcasted_iota(jnp.int32, (8 * SLOT, IMG), 0) == place, 1.0, 0.0
    ).astype(BF)
    c_feat.wait()
    fsend[...] = jnp.dot(perm[...], feat[...], preferred_element_type=F32).astype(BF)

    def f_copy(delta):
        dx, dy, dz = offset_of(delta, core)
        row = pl.multiple_of((core * 8 + delta) * SLOT, SLOT)
        return remote(
            fsend.at[pl.ds(delta * SLOT, SLOT)], fr.at[pl.ds(row, SLOT)],
            f_ss.at[delta], f_rs.at[delta], dest_of(x + dx, y + dy, z + dz, core),
        )

    for delta in (4, 3, 5, 2, 6, 1, 7):
        f_copy(delta).start()
    @pl.when(is_relay)
    def _():
        for c, fan in ((1, fan1), (0, fan0)):

            @pl.when(core == c)
            def _():
                for slot in range(2 - c):
                    hop_copy(slot).wait_recv()
                    for n in range(3):
                        if fan[n][0] == slot:
                            fan_copy(n, *fan[n]).start()

    own0 = pl.multiple_of(core * 8 * SLOT, SLOT)
    fr[pl.ds(own0, SLOT), :] = fsend[0:SLOT, :]

    scale, shift = scale_ref[0], shift_ref[0]
    c_img.wait()
    c_txt.wait()

    def pairs(first, rows, match):
        block = txt[pl.ds(first, rows), :]
        logits = scale * lax.dot_general(
            block, img[...], (((1,), (1,)), ((), ())), preferred_element_type=F32
        ) + shift
        if match:
            hit = lax.broadcasted_iota(jnp.int32, (rows, IMG), 0) == (
                lax.broadcasted_iota(jnp.int32, (rows, IMG), 1) // 2
            )
            labels = jnp.where(hit, 1.0, -1.0)
            arg = -labels * logits
            amount = -scale * labels
        else:
            arg = logits
            amount = scale
        small = jnp.exp(-jnp.abs(arg))
        loss = jnp.maximum(arg, 0.0) + jnp.log1p(small)
        inv = 1.0 / (1.0 + small)
        sig = jnp.where(arg >= 0.0, inv, small * inv)
        wts[pl.ds(first, rows), :] = (amount * sig).astype(BF)
        return jnp.sum(loss, axis=0, keepdims=True)

    loss = pairs(0, TXT, True)

    txt_copy(2).wait_recv()

    @pl.when(at >= 2)
    def _():
        handed.start()

    for delta in (1, 7, 2, 6, 3, 5, 4):
        f_copy(delta).wait_recv()
    half_rows = pl.ds(own0, 8 * SLOT)
    ff = remote(fr.at[half_rows], fr.at[half_rows], ff_ss, ff_rs, sibling)
    ff.start()

    txt_copy(1).wait_recv()
    txt_copy(3).wait_recv()
    loss_ref[...] = (loss + pairs(TXT, (STEPS - 1) * TXT, False)).reshape(IMG)

    picked = lax.dot_general(
        perm[...], wts[...], (((1,), (1,)), ((), ())), preferred_element_type=F32
    ).astype(BF)
    gsend[...] = jnp.dot(picked, txt[...], preferred_element_type=F32).astype(BF)

    def g_copy(delta, half):
        dx, dy, dz = offset_of(delta, core)
        row = pl.multiple_of((core * 8 + delta) * SLOT, SLOT)
        dev = sibling if delta == 0 else dest_of(x + dx, y + dy, z + dz, half)
        col = half * HALF
        if delta == 0:
            col = pl.multiple_of(other * HALF, HALF)
        return remote(
            gsend.at[pl.ds(delta * SLOT, SLOT), pl.ds(col, HALF)], gr.at[pl.ds(row, SLOT)],
            g_ss.at[delta, half], g_rs.at[core, delta], dev,
        )

    g_list = [(delta, half) for delta in (4, 3, 5, 2, 6, 1, 7) for half in range(2)] + [(0, 0)]
    for delta, half in g_list:
        g_copy(delta, half).start()
    gr[pl.ds(own0, SLOT), :] = gsend[0:SLOT, pl.ds(pl.multiple_of(core * HALF, HALF), HALF)]

    sums = jnp.dot(wts[TXT:, :], img[...], preferred_element_type=F32)
    tgs[...] = sums.astype(BF)

    def tg_copy(s):
        rows = pl.ds((s - 1) * TXT, TXT)
        return remote(tgs.at[rows], tgr.at[rows], tg_ss.at[s - 1], tg_rs.at[s - 1], along(-s))

    back = ((0, 1, 0, 1), (0, 2, 0, 0), (0, 3, 2, 0), (1, 2, 1, 1), (1, 3, 1, 0), (2, 3, 2, 1))

    def back_out(s, slot, c, j):
        return remote(
            tgs.at[pl.ds((s - 1) * TXT, TXT), pl.ds(j * PIECE, PIECE)], back_a.at[slot],
            tg_ss.at[s - 1], back_ar.at[slot], relay_of(j, z + 2 * c - 1, c),
        )

    for i, s, slot, c in back:

        @pl.when(is_first[i])
        def _():
            for j in range(8):
                back_out(s, slot, c, j).start()

    for s in range(1, STEPS):

        @pl.when(inside(-s))
        def _():
            tg_copy(s).start()

    tgrad_ref[...] = jnp.dot(wts[0:TXT, :], img[...], preferred_element_type=F32)

    ff_in = remote(
        fr.at[pl.ds(pl.multiple_of(other * 8 * SLOT, SLOT), 8 * SLOT)],
        fr.at[pl.ds(pl.multiple_of(other * 8 * SLOT, SLOT), 8 * SLOT)],
        ff_ss, ff_rs, sibling,
    )
    ff_in.wait_recv()
    ft[...] = jnp.transpose(fr[...])

    def g_arrival(cs, delta):
        rows = pl.ds((cs * 8 + delta) * SLOT, SLOT)
        return remote(gr.at[rows], gr.at[rows], g_ss.at[0, 1], g_rs.at[cs, delta], sibling)

    for delta in (1, 7, 2, 6, 3, 5, 4):
        for cs in range(2):
            g_arrival(cs, delta).wait_recv()
    remote(gr.at[pl.ds(0, SLOT)], gr.at[pl.ds(0, SLOT)], g_ss.at[0, 1], g_rs.at[other, 0], sibling).wait_recv()

    def quarter(q, k):
        col = pl.multiple_of(lax.rem(q + NX, NX) * QUART, QUART)
        lo, hi = CHUNKS[k]
        return jnp.dot(ft[lo:hi, :], gr[:, pl.ds(col, QUART)], preferred_element_type=F32)

    def s1_copy(k, i):
        step = (2 * sign, 1, -1)[i]
        lo, hi = CHUNKS[k]
        rows = pl.ds(lo, hi - lo)
        return remote(
            s1s.at[i, rows], s1r.at[i, rows], s1_ss.at[k, i], s1_rs.at[k, i],
            dest_of(x + step, y + step, z - step, core),
        )

    for k in range(2):
        lo, hi = CHUNKS[k]
        for i, q in enumerate((x + 2, x + 1, x - 1)):
            s1s[i, lo:hi, :] = quarter(q, k).astype(BF)
            s1_copy(k, i).start()

    back_copy = remote(back_a, back_b, back_bs, back_br, dest_of(x, y, z + ZLO - lean, core))

    @pl.when(is_relay)
    def _():
        for slot in range(3):
            remote(back_a.at[slot], back_a.at[slot], back_bs, back_ar.at[slot], sibling).wait_recv()
        back_copy.start()

    target_z = residue + 8 * core

    def s2_copy(k, yt):
        row = pl.multiple_of(z * 16, 16)
        lo, hi = CHUNKS[k]
        cols = pl.ds(lo, hi - lo)
        return remote(
            s2s.at[pl.ds(yt * 16, 16), cols], s2r.at[pl.ds(row, 16), cols], s2_ss.at[k, yt], s2_rs.at[k, z],
            dest_of(x, yt, target_z, core),
        )

    mines = [quarter(x, k) for k in range(2)]
    for k in range(2):
        lo, hi = CHUNKS[k]
        mine = mines[k]
        for i in (1, 2, 0):
            s1_copy(k, i).wait_recv()
            mine = mine + s1r[i, lo:hi, :].astype(F32)
        s2s[:, lo:hi] = jnp.transpose(mine).astype(BF)
        for yt in range(NY):
            here = jnp.logical_and(to_self, y == yt)

            @pl.when(jnp.logical_not(here))
            def _():
                s2_copy(k, yt).start()

            @pl.when(here)
            def _():
                s2r[pl.ds(pl.multiple_of(z * 16, 16), 16), lo:hi] = s2s[yt * 16 : yt * 16 + 16, lo:hi]

    home1 = ((0, 0, 1), (1, 0, 2), (2, 0, 3))
    home0 = ((0, 1, 2), (1, 1, 3), (2, 2, 3))

    def home_copy(slot, i, s):
        return remote(
            back_b.at[slot], tgr.at[pl.ds((s - 1) * TXT, TXT), piece_cols],
            back_cs.at[slot], tg_rs.at[s - 1], last_dev(i, z),
        )

    @pl.when(is_relay)
    def _():
        back_copy.wait_recv()
        for c, home in ((1, home1), (0, home0)):

            @pl.when(core == c)
            def _():
                for args in home:
                    home_copy(*args).start()

    for s in range(1, STEPS):
        tg_copy(s).wait_recv()
    tgrad_ref[...] += (
        tgr[0:TXT, :].astype(F32) + tgr[TXT : 2 * TXT, :].astype(F32) + tgr[2 * TXT :, :].astype(F32)
    )

    def fin_copy(k):
        lo, hi = CHUNKS[k]
        cols = pl.ds(lo, hi - lo)
        return remote(
            fin_s.at[pl.ds(pl.multiple_of(other * 8, 8), 8), cols], fin_r.at[:, cols], fin_ss.at[k], fin_rs.at[k], sibling
        )

    @pl.when(core == zh)
    def _():
        for k in range(2):
            lo, hi = CHUNKS[k]
            for zs in range(NZ):

                @pl.when(jnp.logical_or(source_y(zs) != y, zs != z))
                def _():
                    block = s2r.at[pl.ds(zs * 16, 16), pl.ds(lo, hi - lo)]
                    remote(block, block, s2_ss.at[k, 0], s2_rs.at[k, zs], sibling).wait_recv()

            total = s2r[0:16, lo:hi].astype(F32)
            for zs in range(1, NZ):
                total = total + s2r[zs * 16 : zs * 16 + 16, lo:hi].astype(F32)
            fin_s[:, lo:hi] = total
            fin_copy(k).start()
        egrad_ref[0] = fin_s[pl.ds(pl.multiple_of(core * 8, 8), 8), :]
        for k in range(2):
            fin_copy(k).wait_send()

    @pl.when(core != zh)
    def _():
        for k in range(2):
            fin_copy(k).wait_recv()
        egrad_ref[0] = fin_r[...]

    for s, flag in sends:

        @pl.when(flag)
        def _():
            txt_copy(s).wait_send()

        tg_copy(s).wait_send()

    @pl.when(at >= 2)
    def _():
        handed.wait_send()

    @pl.when(at >= RUN - 3)
    def _():
        remote(txt_hbm, txt.at[pl.ds(0, TXT)], rel_ss, txt_rs.at[0], sibling).wait_send()

    @pl.when(is_relay)
    def _():
        hop_copy(0).wait_send()

        @pl.when(core == 0)
        def _():
            hop_copy(1).wait_send()

        for n in range(3):
            fan_copy(n, *fan1[0]).wait_send()
            home_copy(*home1[n]).wait_send()
        back_copy.wait_send()

    for delta in range(1, 8):
        f_copy(delta).wait_send()
    ff.wait_send()
    for delta, half in g_list:
        g_copy(delta, half).wait_send()
    for k in range(2):
        for i in range(3):
            s1_copy(k, i).wait_send()
        for yt in range(NY):

            @pl.when(jnp.logical_not(jnp.logical_and(to_self, y == yt)))
            def _():
                s2_copy(k, yt).wait_send()


def on_device(images, texts, feats, ids, scale, shift):
    vmem, smem, dma = pltpu.VMEM, pltpu.SMEM, pltpu.SemaphoreType.DMA
    loss, tgrad, egrad = pl.pallas_call(
        kernel,
        out_shape=(
            jax.ShapeDtypeStruct((IMG,), F32),
            jax.ShapeDtypeStruct((TXT, EMB), F32),
            jax.ShapeDtypeStruct((1, 8, FEAT), F32),
        ),
        in_specs=[
            pl.BlockSpec(memory_space=pl.ANY),
            pl.BlockSpec(memory_space=pl.ANY),
            pl.BlockSpec(memory_space=pl.ANY),
            pl.BlockSpec(memory_space=vmem),
            pl.BlockSpec(memory_space=smem),
            pl.BlockSpec(memory_space=smem),
        ],
        out_specs=(
            pl.BlockSpec(memory_space=vmem),
            pl.BlockSpec(memory_space=vmem),
            pl.BlockSpec(memory_space=vmem),
        ),
        scratch_shapes=[
            vmem((IMG, EMB), BF),
            vmem((IMG, FEAT), BF),
            vmem((STEPS * TXT, EMB), BF),
            vmem((8 * SLOT, IMG), BF),
            vmem((STEPS * TXT, IMG), BF),
            vmem((8 * SLOT, FEAT), BF),
            vmem((16 * SLOT, FEAT), BF),
            vmem((FEAT, 16 * SLOT), BF),
            vmem((8 * SLOT, EMB), BF),
            vmem((16 * SLOT, HALF), BF),
            vmem(((STEPS - 1) * TXT, EMB), BF),
            vmem(((STEPS - 1) * TXT, EMB), BF),
            vmem((3, FEAT, QUART), BF),
            vmem((3, FEAT, QUART), BF),
            vmem((QUART, FEAT), BF),
            vmem((NZ * 16, FEAT), BF),
            vmem((16, FEAT), F32),
            vmem((8, FEAT), F32),
            vmem((2, TXT, PIECE), BF),
            vmem((2, TXT, PIECE), BF),
            vmem((3, TXT, PIECE), BF),
            vmem((3, TXT, PIECE), BF),
            dma((3,)),
            dma((STEPS - 1,)),
            dma((STEPS - 1,)),
            dma((8,)),
            dma((8,)),
            dma,
            dma,
            dma((8, 2)),
            dma((2, 8)),
            dma((STEPS - 1,)),
            dma((STEPS - 1,)),
            dma((2, 3)),
            dma((2, 3)),
            dma((2, NY)),
            dma((2, NZ)),
            dma((2,)),
            dma((2,)),
            dma,
            dma,
            dma((2,)),
            dma((2,)),
            dma((2,)),
            dma((2,)),
            dma((3,)),
            dma((3,)),
            dma,
            dma,
            dma((3,)),
        ],
        compiler_params=pltpu.CompilerParams(
            collective_id=0, has_side_effects=True, vmem_limit_bytes=VLIM
        ),
        cost_estimate=pl.CostEstimate(flops=2_000_000_000, bytes_accessed=8_000_000, transcendentals=300_000),
    )(images, texts, feats, ids.reshape(1, IMG), scale, shift)
    return loss, tgrad, egrad


def solution(mesh):
    both = P(("dp", "expert"), None)
    return jax.shard_map(
        on_device,
        mesh=mesh,
        in_specs=(both, both, both, both, P(), P()),
        out_specs=(P(("dp", "expert")), both, P("expert", "dp", None)),
        check_vma=False,
    )
```
